32 devices in a mesh: seq: 8 (over y, x, core), exp: 4 (over z).
Axes of the slice: x: 2, y: 2, z: 4, core: 2. Of those that a mesh axis runs over, the one named last changes fastest.
Arguments:
- tokens: bfloat16 [16, 2048, 768], P('exp', 'seq'), may hold values from -6 to 6
- cotangent: bfloat16 [16, 2048, 768], P('exp', 'seq'), may hold values from -6 to 6
- lengths: int32 [4, 4], P('exp'), may hold values from 1 to 2048, 5120 in all within a row
- routes: int32 [16, 2048, 2], P('exp', 'seq'), may hold values from 0 to 7, all different within a row
- gate_weights: float32 [16, 2048, 2], P('exp', 'seq'), may hold values from 0.5 to 1.5
- norm_gains: float32 [768, 2], P(('seq', 'exp'))
- gains_first: float32 [768, 2], P(('seq', 'exp')), may hold values from -160 to 160
- gains_second: float32 [768, 2], P(('seq', 'exp')), may hold values from 49.152 to 196.608
- input_weight: float32 [768, 2304], P(('seq', 'exp'))
- input_first: float32 [768, 2304], P(('seq', 'exp')), may hold values from -80 to 80
- input_second: float32 [768, 2304], P(('seq', 'exp')), may hold values from 17.69472 to 70.77888
- output_weight: float32 [768, 768], P(('seq', 'exp'))
- output_first: float32 [768, 768], P(('seq', 'exp')), may hold values from -40 to 40
- output_second: float32 [768, 768], P(('seq', 'exp')), may hold values from 4.42368 to 17.69472
- frozen_in: bfloat16 [4, 768, 3072], P('exp', 'seq'), may hold values from -0.21875 to 0.21875
- frozen_out: bfloat16 [4, 3072, 768], P('exp', 'seq'), may hold values from -0.109375 to 0.109375
- expert_in: float32 [4, 768, 3072], P('exp', 'seq')
- inner_first: float32 [4, 768, 3072], P('exp', 'seq'), may hold values from -32 to 32
- inner_second: float32 [4, 768, 3072], P('exp', 'seq'), may hold values from 2.21184 to 8.84736
- expert_out: float32 [4, 3072, 768], P('exp', 'seq')
- outer_first: float32 [4, 3072, 768], P('exp', 'seq'), may hold values from -24 to 24
- outer_second: float32 [4, 3072, 768], P('exp', 'seq'), may hold values from 1.10592 to 4.42368
Outputs:
- block_output: bfloat16 [16, 2048, 768], P('exp', 'seq')
- token_grad: float32 [16, 2048, 768], P('exp', 'seq')
- gains_grad: float32 [768, 2], P(('seq', 'exp'))
- gains_moment: float32 [768, 2], P(('seq', 'exp'))
- gains_square: float32 [768, 2], P(('seq', 'exp'))
- gains_new: float32 [768, 2], P(('seq', 'exp'))
- input_grad: float32 [768, 2304], P(('seq', 'exp'))
- input_moment: float32 [768, 2304], P(('seq', 'exp'))
- input_square: float32 [768, 2304], P(('seq', 'exp'))
- input_new: float32 [768, 2304], P(('seq', 'exp'))
- output_grad: float32 [768, 768], P(('seq', 'exp'))
- output_moment: float32 [768, 768], P(('seq', 'exp'))
- output_square: float32 [768, 768], P(('seq', 'exp'))
- output_new: float32 [768, 768], P(('seq', 'exp'))
- inner_grad: float32 [4, 768, 3072], P('exp', 'seq')
- inner_moment: float32 [4, 768, 3072], P('exp', 'seq')
- inner_square: float32 [4, 768, 3072], P('exp', 'seq')
- inner_new: float32 [4, 768, 3072], P('exp', 'seq')
- outer_grad: float32 [4, 3072, 768], P('exp', 'seq')
- outer_moment: float32 [4, 3072, 768], P('exp', 'seq')
- outer_square: float32 [4, 3072, 768], P('exp', 'seq')
- outer_new: float32 [4, 3072, 768], P('exp', 'seq')
- matrix_norms: float32 [12, 2], replicated
- trust_ratios: float32 [12], replicated
- routed_counts: int32 [8], replicated
The draws below stay inside these ranges and needn't reach their ends.
Inputs may be any that keep to these rules, and one draw needn't show every extreme that they name: `lengths`: each row sums to 5120 and its longest entry is 2048. `routes`: the two experts of a token differ.
All inputs are finite; a program needn't handle non-finite values.
Results may differ from the reference program's by a relative error of at most 0.03.
Values may be sent and summed in bfloat16 or wider, within the bound.
No kernel may reach another device: no remote copies, remote signals or barrier semaphores. Data moves between devices by JAX's collectives and lax.ppermute only.
A program may use at most 320 MiB of HBM per device.

```python
import math
import jax
import jax.numpy as jnp
import numpy as np
from jax import lax

D = 768
HEADS = 12
HEAD_DIM = 64
FF = 3072
SEQ_LEN = 2048
SEQS_DEV = 4
STEP = 10
EXPERTS = 8
HALF = 4
POS_DEV = 256
TOK_DEV = 1024
SEQS = 16
TOKENS = 32768
CAP = 256
N_SEQ = 8
N_EXP = 4


def row_factor(key, rows, rise, spread):
    place = jnp.arange(rows, dtype=jnp.float32) / rows
    rough = jax.random.uniform(key, (rows,), jnp.float32, 0.7, 1.4)
    return (1.0 + rise * place) * rough / spread


def draw_norm_gains(key, part):
    key = jax.random.fold_in(key, 5)
    place = jnp.arange(D, dtype=jnp.float32)[:, None] / D
    rough = jax.random.uniform(key, (D, 2), jnp.float32, 0.8, 1.25)
    return (0.5 + place) * rough


def draw_input_weight(key, part):
    key = jax.random.fold_in(key, 11)
    key_base, key_rows = jax.random.split(key)
    shape = (D, 3 * D)
    base = jax.random.normal(key_base, shape, jnp.float32)
    factor = row_factor(key_rows, D, 2.0, 2.22)
    return base * factor[:, None] * D ** (-0.5)


def draw_output_weight(key, part):
    key = jax.random.fold_in(key, 13)
    key_base, key_rows = jax.random.split(key)
    shape = (D, D)
    base = jax.random.normal(key_base, shape, jnp.float32)
    factor = row_factor(key_rows, D, 2.0, 2.22)
    return base * factor[:, None] * (D // 8) ** (-0.5)


def draw_expert_in(key, part):
    key = jax.random.fold_in(key, 17)
    key_base, key_rows = jax.random.split(key)
    shape = (HALF, D, FF)
    base = jax.random.normal(key_base, shape, jnp.float32)
    factor = row_factor(key_rows, D, 2.0, 2.22)
    return base * factor[None, :, None] * D ** (-0.5)


def draw_expert_out(key, part):
    key = jax.random.fold_in(key, 19)
    key_base, key_rows = jax.random.split(key)
    shape = (HALF, FF, D)
    base = jax.random.normal(key_base, shape, jnp.float32)
    factor = row_factor(key_rows, FF, 2.0, 2.22)
    return base * factor[None, :, None] * FF ** (-0.5)


def shard_levels(key, shape, cuts, smallest, largest):
    level, own = 1.0, jax.random.fold_in(key, 6)
    for position, blocks in cuts:
        heights = jnp.exp(jax.random.uniform(jax.random.fold_in(own, position), (blocks,), jnp.float32, smallest / len(cuts), largest / len(cuts)))
        level = level * jnp.repeat(heights, shape[position] // blocks).reshape([-1 if axis == position else 1 for axis in range(len(shape))])
    return level


def picks_of(own_key, rows, number_of, top, lift):
    order = jax.random.permutation(jax.random.fold_in(own_key, 1), number_of)
    favour = order
    for power in range(3):
        favour = favour * favour // number_of
    favour = favour * lift // number_of
    lots = jax.random.randint(jax.random.fold_in(own_key, 2), (rows, number_of), 0, 4096) + favour
    fixed_rows = jax.random.permutation(jax.random.fold_in(own_key, 3), rows)[jnp.arange(number_of) % rows]
    lots = jnp.where(jnp.arange(rows)[:, None] == fixed_rows[None, :], 1 << 14, lots)
    merit = lots * number_of + jnp.arange(number_of)
    return lax.top_k(merit.astype(jnp.int32), top)[1].astype(jnp.int32)


def length_profile(amount, total, bound, lean):
    loads = [(1 << 20) // math.isqrt(grade ** lean) + 1 for grade in range(2, amount + 1)]
    surplus, holding = total - bound - (amount - 1), [1] * (amount - 1)
    while surplus > 0:
        movable = [i for i in range(amount - 1) if holding[i] < bound]
        whole, left = sum([loads[i] for i in movable]), surplus
        for i in movable:
            more = min(bound - holding[i], max(1, left * loads[i] // whole), surplus)
            holding[i] = holding[i] + more
            surplus = surplus - more
    return np.array([bound] + holding)


def uneven(key, amount, total, most, lean):
    if amount == 2:
        one = jax.random.randint(key, (), max(1, total - most), min(most, total - 1) + 1)
        return jnp.stack([one, total - one])
    tallies = jnp.asarray(length_profile(amount, total, most, lean), jnp.int32)
    twos = (amount - 1) // 2
    donor, taker = tallies[1:1 + 2 * twos:2], tallies[2:2 + 2 * twos:2]
    room = jnp.minimum(donor - 1, most - taker)
    passed = jax.random.randint(jax.random.fold_in(key, 1), (twos,), 0, 1 << 20) % (room + 1)
    tallies = tallies.at[1:1 + 2 * twos:2].set(donor - passed).at[2:2 + 2 * twos:2].set(taker + passed)
    return tallies[jax.random.permutation(jax.random.fold_in(key, 2), amount)]


def gaussian(own_key, shape, deviation, limit, cuts=(), held_as=jnp.bfloat16):
    values = deviation * jax.random.normal(own_key, shape, jnp.float32)
    if cuts:
        values = values * shard_levels(own_key, shape, cuts, -0.22, 0.18)
    return jnp.clip(values, -limit, limit).astype(held_as)


def setup_inputs(seed: int = 0) -> dict:
    key_list = jax.random.split(jax.random.key(seed), 23)
    tokens = gaussian(key_list[0], (SEQS, SEQ_LEN, D), 1.0, 6.0, ((0, 4), (1, 8)))
    cotangent = gaussian(key_list[1], (SEQS, SEQ_LEN, D), 1.0, 6.0, ((0, 4), (1, 8)))
    lengths = jax.vmap(lambda own: uneven(own, SEQS_DEV, SEQ_LEN * (SEQS_DEV + 1) // 2, SEQ_LEN, 2))(jax.random.split(key_list[2], N_EXP)).reshape((N_EXP, SEQS_DEV)).astype(jnp.int32)
    routes = picks_of(key_list[3], SEQS * SEQ_LEN, EXPERTS, 2, 2048).reshape((SEQS, SEQ_LEN, 2))
    gate_weights = jnp.clip(0.5 + 1.0 * jax.random.uniform(key_list[4], (SEQS, SEQ_LEN, 2), jnp.float32) ** shard_levels(key_list[4], (SEQS, SEQ_LEN, 2), ((0, 4), (1, 8)), -0.2, 0.2), 0.5, 1.5)
    norm_gains = draw_norm_gains(jax.random.fold_in(key_list[22], 71), 0)
    gains_first = gaussian(key_list[6], (D, 2), (0.14 * TOKENS ** 0.5), 160.0, ((0, 32),), jnp.float32)
    gains_second = jnp.clip(jnp.exp(math.log(196.608) - 1.3862944 * jax.random.uniform(key_list[7], (D, 2), jnp.float32) ** shard_levels(key_list[7], (D, 2), ((0, 32),), -0.2, 0.2)), 49.152, 196.608)
    input_weight = draw_input_weight(jax.random.fold_in(key_list[22], 71), 0)
    input_first = gaussian(key_list[9], (D, 3 * D), (0.08 * TOKENS ** 0.5), 80.0, ((0, 32),), jnp.float32)
    input_second = jnp.clip(jnp.exp(math.log(70.77888) - 1.3862944 * jax.random.uniform(key_list[10], (D, 3 * D), jnp.float32) ** shard_levels(key_list[10], (D, 3 * D), ((0, 32),), -0.2, 0.2)), 17.69472, 70.77888)
    output_weight = draw_output_weight(jax.random.fold_in(key_list[22], 71), 0)
    output_first = gaussian(key_list[12], (D, D), (0.04 * TOKENS ** 0.5), 40.0, ((0, 32),), jnp.float32)
    output_second = jnp.clip(jnp.exp(math.log(17.69472) - 1.3862944 * jax.random.uniform(key_list[13], (D, D), jnp.float32) ** shard_levels(key_list[13], (D, D), ((0, 32),), -0.2, 0.2)), 4.42368, 17.69472)
    frozen_in = gaussian(key_list[14], (HALF, D, FF), D ** -0.5, 0.21875, ((0, 4), (1, 8)))
    frozen_out = gaussian(key_list[15], (HALF, FF, D), FF ** -0.5, 0.109375, ((0, 4), (1, 8)))
    expert_in = draw_expert_in(jax.random.fold_in(key_list[22], 71), 0)
    inner_first = gaussian(key_list[17], (HALF, D, FF), (0.08 * (TOKENS // EXPERTS) ** 0.5), 32.0, ((0, 4), (1, 8)), jnp.float32)
    inner_second = jnp.clip(jnp.exp(math.log(8.84736) - 1.3862944 * jax.random.uniform(key_list[18], (HALF, D, FF), jnp.float32) ** shard_levels(key_list[18], (HALF, D, FF), ((0, 4), (1, 8)), -0.2, 0.2)), 2.21184, 8.84736)
    expert_out = draw_expert_out(jax.random.fold_in(key_list[22], 71), 0)
    outer_first = gaussian(key_list[20], (HALF, FF, D), (0.06 * (TOKENS // EXPERTS) ** 0.5), 24.0, ((0, 4), (1, 8)), jnp.float32)
    outer_second = jnp.clip(jnp.exp(math.log(4.42368) - 1.3862944 * jax.random.uniform(key_list[21], (HALF, FF, D), jnp.float32) ** shard_levels(key_list[21], (HALF, FF, D), ((0, 4), (1, 8)), -0.2, 0.2)), 1.10592, 4.42368)
    return {"tokens": tokens, "cotangent": cotangent, "lengths": lengths, "routes": routes, "gate_weights": gate_weights, "norm_gains": norm_gains, "gains_first": gains_first, "gains_second": gains_second, "input_weight": input_weight, "input_first": input_first, "input_second": input_second, "output_weight": output_weight, "output_first": output_first, "output_second": output_second, "frozen_in": frozen_in, "frozen_out": frozen_out, "expert_in": expert_in, "inner_first": inner_first, "inner_second": inner_second, "expert_out": expert_out, "outer_first": outer_first, "outer_second": outer_second}


@jax.custom_vjp
def low(v):
    return lax.optimization_barrier(v.astype(jnp.bfloat16)).astype(jnp.float32)

@jax.custom_vjp
def low_back(v):
    return v

def low_keep(v):
    return (low(v), None)

def low_pass(kept, grad):
    return (grad,)

def back_keep(v):
    return (v, None)

def back_low(kept, grad):
    return (low(grad),)
low.defvjp(low_keep, low_pass)
low_back.defvjp(back_keep, back_low)
norm_eps = 1e-06
beta_one = 0.9
beta_two = 0.999
lamb_eps = 1e-06
decay_rate = 0.01
learn_rate = 0.3
masked_score = -1e+30
highest = lax.Precision.HIGHEST

def rms_norm(values, gain):
    factor = lax.rsqrt(lax.optimization_barrier(jnp.mean(values * values, axis=-1, keepdims=True)) + norm_eps)
    return values * factor * gain

def device_order(array):
    extra = array.shape[2:]
    split = array.reshape((N_EXP, SEQS_DEV, N_SEQ, POS_DEV) + extra)
    moved = jnp.moveaxis(split, 2, 0)
    return moved.reshape((N_SEQ * N_EXP, SEQS_DEV * POS_DEV) + extra)

def routing(lengths, routes):
    devices = N_SEQ * N_EXP
    seq_lengths = lengths.reshape(SEQS)
    live_mask = jnp.arange(SEQ_LEN, dtype=jnp.int32)[None, :] < seq_lengths[:, None]
    token_ids = jnp.arange(SEQS * SEQ_LEN, dtype=jnp.int32).reshape(SEQS, SEQ_LEN)
    pair_routes = device_order(routes).reshape(devices, TOK_DEV * 2)
    pair_live = jnp.repeat(device_order(live_mask), 2, axis=1)
    pair_tokens = jnp.repeat(device_order(token_ids), 2, axis=1)
    pair_ids = pair_tokens * 2 + jnp.tile(jnp.arange(2, dtype=jnp.int32), TOK_DEV)[None, :]
    expert_hits = (pair_routes[:, :, None] == jnp.arange(EXPERTS, dtype=jnp.int32)[None, None, :]) & pair_live[:, :, None]
    running = jnp.cumsum(expert_hits.astype(jnp.int32), axis=1) - 1
    pair_rank = lax.optimization_barrier(jnp.sum(jnp.where(expert_hits, running, 0), axis=2))
    pair_kept = pair_live & (pair_rank < CAP)
    device = jnp.arange(devices, dtype=jnp.int32)[:, None]
    pair_slot = (pair_routes * devices + device) * CAP + pair_rank
    total_slots = EXPERTS * devices * CAP
    slot_owner = jnp.full((total_slots,), -1, jnp.int32).at[jnp.where(pair_kept, pair_slot, total_slots).reshape(-1)].set(pair_tokens.reshape(-1), mode='drop')
    token_slot = jnp.zeros((SEQS * SEQ_LEN * 2,), jnp.int32).at[pair_ids.reshape(-1)].set(jnp.where(pair_kept, pair_slot, 0).reshape(-1))
    token_keep = jnp.zeros((SEQS * SEQ_LEN * 2,), jnp.int32).at[pair_ids.reshape(-1)].set(pair_kept.astype(jnp.int32).reshape(-1))
    counts = lax.optimization_barrier(jnp.sum((expert_hits & pair_kept[:, :, None]).astype(jnp.int32), axis=(0, 1)))
    return (token_slot.reshape(-1, 2), token_keep.reshape(-1, 2), slot_owner, counts)

def attend(inputs):
    queries, key_block, value_block, length = inputs
    positions = jnp.arange(SEQ_LEN, dtype=jnp.int32)
    allowed = (positions[None, :] <= positions[:, None]) & (positions[None, :] < length)
    scores = jnp.einsum('qhd,khd->hqk', queries, key_block, precision=highest) * HEAD_DIM ** (-0.5)
    scores = jnp.where(allowed[None], low_back(scores), masked_score)
    weights = low(jax.nn.softmax(scores, axis=-1))
    return jnp.einsum('hqk,khd->qhd', weights, value_block, precision=highest)

def lamb_update(weight, grad, first, second, decay):
    first_new = beta_one * first + (1.0 - beta_one) * grad
    second_new = beta_two * second + (1.0 - beta_two) * grad * grad
    update = first_new / (1.0 - beta_one ** STEP) / (jnp.sqrt(second_new / (1.0 - beta_two ** STEP)) + lamb_eps) + decay * weight
    return (first_new, second_new, update)

def reference(tokens, cotangent, lengths, routes, gate_weights, norm_gains, gains_first, gains_second, input_weight, input_first, input_second, output_weight, output_first, output_second, frozen_in, frozen_out, expert_in, inner_first, inner_second, expert_out, outer_first, outer_second):
    token_slot, token_keep, slot_owner, counts = routing(lengths, routes)
    gate_pair = jnp.where(token_keep == 1, gate_weights.reshape(-1, 2), 0.0)
    seq_lengths = lengths.reshape(SEQS)
    frozen_in_f = frozen_in.astype(jnp.float32)
    frozen_out_f = frozen_out.astype(jnp.float32)
    owner_rows = slot_owner.reshape(EXPERTS, -1)

    def forward(tokens_f, gains, weight_input, weight_output, weight_inner, weight_outer):
        gains_low = low(gains)
        first_normed = low(rms_norm(tokens_f, gains_low[:, 0]))
        packed = low_back(low(jnp.dot(first_normed, low(weight_input), precision=highest, preferred_element_type=jnp.float32)))
        parts = packed.reshape(SEQS, SEQ_LEN, 3, HEADS, HEAD_DIM)
        context = lax.map(jax.checkpoint(attend), (parts[:, :, 0], parts[:, :, 1], parts[:, :, 2], seq_lengths))
        context = low_back(low(context.reshape(SEQS * SEQ_LEN, D)))
        branch = low_back(jnp.dot(context, low(weight_output), precision=highest, preferred_element_type=jnp.float32))
        middle = tokens_f + branch
        second_normed = low(rms_norm(middle, gains_low[:, 1]))
        all_in = jnp.stack([frozen_in_f, low(weight_inner)], axis=1).reshape(EXPERTS, D, FF)
        all_out = jnp.stack([frozen_out_f, low(weight_outer)], axis=1).reshape(EXPERTS, FF, D)

        def expert(inputs):
            weight_in, weight_out, owners = inputs
            filled = (owners >= 0)[:, None]
            taken = low_back(jnp.where(filled, jnp.take(second_normed, jnp.maximum(owners, 0), axis=0), 0.0))
            hidden = low_back(jnp.dot(taken, weight_in, precision=highest, preferred_element_type=jnp.float32))
            active = low(jax.nn.gelu(hidden))
            return low_back(low(jnp.dot(active, weight_out, precision=highest, preferred_element_type=jnp.float32)))
        results = lax.map(jax.checkpoint(expert), (all_in, all_out, owner_rows)).reshape(-1, D)
        picked = jnp.take(results, token_slot, axis=0)
        mixture = lax.optimization_barrier(jnp.sum(picked * gate_pair[:, :, None], axis=1))
        return middle + mixture
    tokens_f = tokens.reshape(SEQS * SEQ_LEN, D).astype(jnp.float32)
    result, pullback = jax.vjp(forward, tokens_f, norm_gains, input_weight, output_weight, expert_in, expert_out)
    grads = pullback(cotangent.reshape(SEQS * SEQ_LEN, D).astype(jnp.float32))
    grad_tokens, grad_gains, grad_input, grad_output, grad_inner, grad_outer = grads
    block_output = result.astype(jnp.bfloat16).reshape(SEQS, SEQ_LEN, D)
    gains_moment, gains_square, gains_update = lamb_update(norm_gains, grad_gains, gains_first, gains_second, 0.0)
    input_moment, input_square, input_update = lamb_update(input_weight, grad_input, input_first, input_second, decay_rate)
    output_moment, output_square, output_update = lamb_update(output_weight, grad_output, output_first, output_second, decay_rate)
    inner_moment, inner_square, inner_update = lamb_update(expert_in, grad_inner, inner_first, inner_second, decay_rate)
    outer_moment, outer_square, outer_update = lamb_update(expert_out, grad_outer, outer_first, outer_second, decay_rate)
    weight_squares = jnp.concatenate([jnp.sum(input_weight * input_weight)[None], jnp.sum(output_weight * output_weight)[None], lax.optimization_barrier(jnp.sum(norm_gains * norm_gains, axis=0)), lax.optimization_barrier(jnp.sum(expert_in * expert_in, axis=(1, 2))), lax.optimization_barrier(jnp.sum(expert_out * expert_out, axis=(1, 2)))])
    update_squares = jnp.concatenate([jnp.sum(input_update * input_update)[None], jnp.sum(output_update * output_update)[None], lax.optimization_barrier(jnp.sum(gains_update * gains_update, axis=0)), lax.optimization_barrier(jnp.sum(inner_update * inner_update, axis=(1, 2))), lax.optimization_barrier(jnp.sum(outer_update * outer_update, axis=(1, 2)))])
    matrix_norms = jnp.sqrt(jnp.stack([weight_squares, update_squares], axis=1))
    trust_ratios = matrix_norms[:, 0] / matrix_norms[:, 1]
    input_new = input_weight - learn_rate * trust_ratios[0] * input_update
    output_new = output_weight - learn_rate * trust_ratios[1] * output_update
    gains_new = norm_gains - learn_rate * trust_ratios[2:4][None, :] * gains_update
    inner_new = expert_in - learn_rate * trust_ratios[4:4 + HALF][:, None, None] * inner_update
    outer_new = expert_out - learn_rate * trust_ratios[4 + HALF:][:, None, None] * outer_update
    token_grad = grad_tokens.reshape(SEQS, SEQ_LEN, D)
    return (block_output, token_grad, grad_gains, gains_moment, gains_square, gains_new, grad_input, input_moment, input_square, input_new, grad_output, output_moment, output_square, output_new, grad_inner, inner_moment, inner_square, inner_new, grad_outer, outer_moment, outer_square, outer_new, matrix_norms, trust_ratios, counts)
```

```python
import functools

import jax
import jax.numpy as jnp
from jax import lax
from jax.experimental import pallas as pl
from jax.experimental.pallas import tpu as pltpu
from jax.sharding import PartitionSpec as P

HEAD_DIM = 64
STEP = 10
LANES = 128
BLOCK = 256

norm_eps = 1e-06
beta_one = 0.9
beta_two = 0.999
lamb_eps = 1e-06
decay_rate = 0.01
learn_rate = 0.3
masked_score = -1e30
gelu_scale = 0.7978845608028654
gelu_cubic = 0.044715
flops_per_us = 1.1535e9

f32 = jnp.float32
bf16 = jnp.bfloat16


def struct(shape, dtype):
    return jax.ShapeDtypeStruct(shape, dtype)


def dot(left, right):
    return jnp.dot(left, right, preferred_element_type=f32)


def dot_rows(left, right):
    return lax.dot_general(left, right, (((1,), (1,)), ((), ())), preferred_element_type=f32)


def run_kernel(
    kernel, grid, in_specs, out_specs, out_shape, scratch, span, *operands, after=(), chosen=()
):
    count = len(chosen) + len(in_specs)

    def run(*refs):
        kernel(*refs[:count], *refs[count + len(after) :])

    waited = [pl.BlockSpec(memory_space=pl.ANY) for _ in after]
    return pl.pallas_call(
        run,
        grid_spec=pltpu.PrefetchScalarGridSpec(
            num_scalar_prefetch=len(chosen),
            grid=grid,
            in_specs=list(in_specs) + waited,
            out_specs=out_specs,
            scratch_shapes=scratch,
        ),
        out_shape=out_shape,
        cost_estimate=pl.CostEstimate(
            flops=int(span * flops_per_us), bytes_accessed=0, transcendentals=0
        ),
        compiler_params=pltpu.CompilerParams(
            dimension_semantics=("arbitrary",) * len(grid),
            vmem_limit_bytes=56 * 1024 * 1024,
        ),
    )(*chosen, *operands, *after)


def whole(shape):
    return pl.BlockSpec(shape, lambda *_: (0,) * len(shape))


scalars = pl.BlockSpec(memory_space=pltpu.SMEM)


class Plan:
    def __init__(self, tokens):
        self.n_seq = lax.axis_size("seq")
        self.n_exp = lax.axis_size("exp")
        self.batch, self.pos, self.width = tokens.shape
        self.tokens = self.batch * self.pos
        self.experts = 2 * self.n_exp
        self.cap = 2 * self.tokens // self.experts
        self.rows = self.n_exp * self.cap
        self.pairs = self.width // LANES
        self.per = self.n_seq // self.batch
        self.chunks = -(-self.pairs // self.per)
        self.length = self.n_seq * self.pos

    def rolled(self, chunk):
        turn = self.batch - chunk % self.batch
        return lambda b: lax.rem(b + turn, self.batch)

    def held(self, chunk):
        return [(k, chunk * self.per + k) for k in range(self.per)]

    def used(self, chunk):
        return min(self.per, self.pairs - chunk * self.per)

    def weight_of(self, chunk):
        return 3 * LANES * self.per * chunk


def routing(plan, routes, live):
    tokens, experts, cap, rows = plan.tokens, plan.experts, plan.cap, plan.rows

    def kernel(route_ref, live_ref, slot_ref, count_ref):
        expert = lax.broadcasted_iota(jnp.int32, (experts, tokens), 0)
        alive = live_ref[...] > 0
        hits = [(route_ref[k : k + 1, :] == expert) & alive for k in range(2)]
        hit = jnp.where(hits[0] | hits[1], 1.0, 0.0)
        before = lax.broadcasted_iota(jnp.int32, (tokens, tokens), 0) < lax.broadcasted_iota(
            jnp.int32, (tokens, tokens), 1
        )
        rank = dot(hit.astype(bf16), jnp.where(before, 1.0, 0.0).astype(bf16))
        kept = rank < cap
        base = (expert % 2) * rows + (expert // 2) * cap + 1
        slot = base.astype(f32) + rank
        for k in range(2):
            own = jnp.sum(jnp.where(hits[k] & kept, slot, 0.0), axis=0, keepdims=True)
            slot_ref[k : k + 1, :] = own.astype(jnp.int32) - 1
        total = jnp.sum(jnp.where(kept, hit, 0.0), axis=1, keepdims=True)
        count_ref[...] = jnp.broadcast_to(total, (experts, LANES))

    return run_kernel(
        kernel,
        (1,),
        [whole((2, tokens)), whole((1, tokens))],
        [whole((2, tokens)), whole((experts, LANES))],
        [struct((2, tokens), jnp.int32), struct((experts, LANES), f32)],
        [],
        4,
        routes,
        live,
    )


def project(plan, tokens, gains, weights, after):
    batch, pos, width, chunks = plan.batch, plan.pos, plan.width, plan.chunks

    def kernel(x_ref, gain_ref, w_ref, *out_refs):
        x = x_ref[0].astype(f32)
        factor = lax.rsqrt(jnp.mean(x * x, axis=-1, keepdims=True) + norm_eps)
        normed = (x * factor * gain_ref[0:1, :]).astype(bf16)
        for chunk, out_ref in enumerate(out_refs):
            first, used = plan.weight_of(chunk), plan.used(chunk)
            for part in range(3):
                low = first + part * used * LANES
                made = dot(normed, w_ref[:, low : low + used * LANES])
                if part == 0:
                    made = made.astype(bf16).astype(f32) * HEAD_DIM ** (-0.5)
                made = made.astype(bf16)
                for k in range(plan.per):
                    if k < used:
                        out_ref[k, 0, part] = made[:, k * LANES : (k + 1) * LANES]
                    else:
                        out_ref[k, 0, part] = jnp.zeros((pos, LANES), bf16)

    def chunk_spec(chunk):
        turn = plan.rolled(chunk)
        return pl.BlockSpec((plan.per, 1, 3, pos, LANES), lambda b: (0, turn(b), 0, 0, 0))

    return list(
        run_kernel(
            kernel,
            (batch,),
            [
                pl.BlockSpec((1, pos, width), lambda b: (b, 0, 0)),
                whole((2, width)),
                whole(weights.shape),
            ],
            [chunk_spec(c) for c in range(chunks)],
            [struct((plan.per, batch, 3, pos, LANES), bf16)] * chunks,
            [],
            8,
            tokens,
            gains,
            weights,
            after=after,
        )
    )


def over_seq(values):
    return lax.all_to_all(values, "seq", split_axis=0, concat_axis=0, tiled=True)


def sent(blocks):
    return [shifted(block, k) if k else block for k, block in enumerate(blocks)]


def sent_back(blocks):
    return [shifted(block, len(blocks) - k) if k else block for k, block in enumerate(blocks)]


def shifted(values, distance):
    count = lax.axis_size("exp")
    return lax.ppermute(values, "exp", [(i, (i + distance) % count) for i in range(count)])


def lane_masks():
    lane = lax.broadcasted_iota(jnp.int32, (1, LANES), 1)
    first = jnp.where(lane < HEAD_DIM, 1.0, 0.0)
    return first.astype(bf16), (1.0 - first).astype(bf16)


def allowed_block(key_block, query_block, length):
    key_pos = key_block * BLOCK + lax.broadcasted_iota(jnp.int32, (BLOCK, BLOCK), 0)
    query_pos = query_block * BLOCK + lax.broadcasted_iota(jnp.int32, (BLOCK, BLOCK), 1)
    return (key_pos <= query_pos) & (key_pos < length)


def attend(plan, packed, length, after):
    pos, n_seq = plan.pos, plan.n_seq
    blocks, group = plan.length // BLOCK, BLOCK // pos

    def kernel(length_ref, x_ref, out_ref, log_ref, values_t):
        query_block = pl.program_id(0)
        length = length_ref[0]

        def read(block, part):
            return x_ref[pl.ds(block * group, group), part].reshape(BLOCK, LANES)

        @pl.when(query_block == 0)
        def _():
            for block in range(blocks):
                values_t[block] = read(block, 2).astype(f32).T.astype(bf16)

        query = read(query_block, 0)
        queries = [query * mask for mask in lane_masks()]

        def fold(key_blocks, state, allowed=None):
            scores = [
                [dot_rows(read(block, 1), query) for block in key_blocks] for query in queries
            ]
            after = []
            for head in range(2):
                parts = scores[head]
                if allowed is not None:
                    parts = [jnp.where(allowed, score, masked_score) for score in parts]
                peak = functools.reduce(jnp.maximum, parts)
                peak = jnp.max(peak, axis=0, keepdims=True)
                if state is not None:
                    peak = jnp.maximum(state[head][0], peak)
                weights = [jnp.exp(score - peak) for score in parts]
                total = jnp.sum(sum(weights), axis=0, keepdims=True)
                added = sum(
                    dot(
                        values_t[block, head * HEAD_DIM : (head + 1) * HEAD_DIM, :],
                        weight.astype(bf16),
                    )
                    for block, weight in zip(key_blocks, weights)
                )
                if state is not None:
                    old_peak, old_total, old_sum = state[head]
                    shrink = jnp.exp(old_peak - peak)
                    total = old_total * shrink + total
                    added = old_sum * shrink + added
                after.append((peak, total, added))
            return tuple(after)

        inner = lax.min(query_block, length // BLOCK)
        state = fold([inner], None, allowed_block(inner, query_block, length))
        odd = lax.rem(inner, 2)
        state = lax.fori_loop(0, odd, lambda i, state: fold([i], state), state)
        state = lax.fori_loop(
            0, inner // 2, lambda i, state: fold([odd + 2 * i, odd + 2 * i + 1], state), state
        )
        context = jnp.concatenate([added / total for _, total, added in state], axis=0)
        out_ref[...] = context.T.astype(bf16).reshape(group, pos, LANES)
        for head in range(2):
            peak, total, _ = state[head]
            log_ref[0, head : head + 1, :] = peak + jnp.log(total)

    return run_kernel(
        kernel,
        (blocks,),
        [scalars, whole((n_seq, 3, pos, LANES))],
        [
            pl.BlockSpec((group, pos, LANES), lambda i: (i, 0, 0)),
            pl.BlockSpec((1, 2, BLOCK), lambda i: (i, 0, 0)),
        ],
        [struct((n_seq, pos, LANES), bf16), struct((blocks, 2, BLOCK), f32)],
        [pltpu.VMEM((blocks, LANES, BLOCK), bf16)],
        20,
        length,
        packed,
        after=after,
    )


def attend_back(plan, packed, context, context_grad, log_total, length, after):
    pos, n_seq = plan.pos, plan.n_seq
    blocks, group = plan.length // BLOCK, BLOCK // pos

    def kernel(
        length_ref, x_ref, c_ref, g_ref, log_ref, out_ref, keys_t, queries, grads, delta, query_grad
    ):
        key_block = pl.program_id(0)
        length = length_ref[0]

        def read(ref, block, *part):
            return ref[(pl.ds(block * group, group), *part)].reshape(BLOCK, LANES)

        @pl.when(key_block == 0)
        def _():
            masks = lane_masks()
            for block in range(blocks):
                keys_t[block] = read(x_ref, block, 1).astype(f32).T.astype(bf16)
                query, grad = read(x_ref, block, 0), read(g_ref, block)
                for head in range(2):
                    queries[head, block] = query * masks[head]
                    grads[head, block] = grad * masks[head]
                product = (read(c_ref, block).astype(f32) * grad.astype(f32)).T
                for head in range(2):
                    delta[block, head : head + 1, :] = jnp.sum(
                        product[head * HEAD_DIM : (head + 1) * HEAD_DIM], axis=0, keepdims=True
                    )
                query_grad[block] = jnp.zeros((LANES, BLOCK), f32)

        key = read(x_ref, key_block, 1)
        value = read(x_ref, key_block, 2)
        key_t = keys_t[key_block]

        def fold(masked, query_blocks, state):
            key_grad, value_grad = state
            chains = [(block, head) for block in query_blocks for head in range(2)]
            scores = [dot_rows(key, queries[head, block]) for block, head in chains]
            products = [dot_rows(value, grads[head, block]) for block, head in chains]
            made = []
            for (block, head), score, product in zip(chains, scores, products):
                weight = jnp.exp(score - log_ref[block, head : head + 1, :])
                if masked:
                    weight = jnp.where(allowed_block(key_block, block, length), weight, 0.0)
                value_grad = value_grad + dot(weight.astype(bf16), grads[head, block])
                score_grad = weight * (product - delta[block, head : head + 1, :])
                score_grad = score_grad.astype(bf16)
                key_grad = key_grad + dot(score_grad, queries[head, block])
                made.append(dot(key_t[head * HEAD_DIM : (head + 1) * HEAD_DIM], score_grad))
            for (block, head), part in zip(chains, made):
                query_grad[block, pl.ds(head * HEAD_DIM, HEAD_DIM), :] += part
            return key_grad, value_grad

        zero = jnp.zeros((BLOCK, LANES), f32)

        def store(state):
            for part in range(2):
                out_ref[pl.ds(key_block * group, group), 1 + part] = (
                    state[part].astype(bf16).reshape(group, pos, LANES)
                )

        first = key_block * BLOCK
        inside = first + BLOCK <= length

        @pl.when(inside)
        def _():
            state = fold(True, [key_block], (zero, zero))
            odd = lax.rem(blocks - 1 - key_block, 2)
            state = lax.fori_loop(
                0, odd, lambda i, state: fold(False, [key_block + 1 + i], state), state
            )
            start = key_block + 1 + odd
            pairs = (blocks - start) // 2
            store(
                lax.fori_loop(
                    0,
                    pairs,
                    lambda i, state: fold(False, [start + 2 * i, start + 2 * i + 1], state),
                    state,
                )
            )

        @pl.when(jnp.logical_not(inside) & (first < length))
        def _():
            store(
                lax.fori_loop(
                    key_block, blocks, lambda i, state: fold(True, [i], state), (zero, zero)
                )
            )

        @pl.when(first >= length)
        def _():
            store((zero, zero))

        @pl.when(key_block == blocks - 1)
        def _():
            for block in range(blocks):
                grad = query_grad[block].T * HEAD_DIM ** (-0.5)
                out_ref[block * group : (block + 1) * group, 0] = grad.astype(bf16).reshape(
                    group, pos, LANES
                )

    return run_kernel(
        kernel,
        (blocks,),
        [
            scalars,
            whole((n_seq, 3, pos, LANES)),
            whole((n_seq, pos, LANES)),
            pl.BlockSpec((n_seq, None, pos, LANES), lambda i: (0, context_grad[1], 0, 0)),
            whole((blocks, 2, BLOCK)),
        ],
        whole((n_seq, 3, pos, LANES)),
        struct((n_seq, 3, pos, LANES), bf16),
        [
            pltpu.VMEM((blocks, LANES, BLOCK), bf16),
            pltpu.VMEM((2, blocks, BLOCK, LANES), bf16),
            pltpu.VMEM((2, blocks, BLOCK, LANES), bf16),
            pltpu.VMEM((blocks, 2, BLOCK), f32),
            pltpu.VMEM((blocks, LANES, BLOCK), f32),
        ],
        22,
        length,
        packed,
        context,
        context_grad[0],
        log_total,
        after=after,
    )


def chunk_block(plan, chunk):
    turn = plan.rolled(chunk)
    return pl.BlockSpec((plan.per, 1, plan.pos, LANES), lambda b: (0, turn(b), 0, 0))


def joined_block(plan, chunk, index):
    turn = plan.rolled(chunk)
    block = (plan.per, 1, 1, plan.pos, LANES)
    return pl.BlockSpec(block, lambda b: (0, turn(b), index, 0, 0))


def token_block(plan):
    return pl.BlockSpec((1, plan.pos, plan.width), lambda b: (b, 0, 0))


def combine_heads(plan, tokens, contexts, gains, weights):
    batch, pos, width, chunks = plan.batch, plan.pos, plan.width, plan.chunks

    def kernel(x_ref, gain_ref, w_ref, *refs):
        context_refs, outs = refs[:chunks], refs[chunks:]
        context_ref, middle_ref, normed_ref, scaled_ref = outs
        parts = [
            context_refs[chunk][k, 0, 0]
            for chunk in range(chunks)
            for k, pair in plan.held(chunk)
            if pair < plan.pairs
        ]
        context = jnp.concatenate(parts, axis=1)
        context_ref[0] = context
        x = x_ref[0].astype(f32)
        factor = lax.rsqrt(jnp.mean(x * x, axis=-1, keepdims=True) + norm_eps)
        scaled_ref[0] = (x * factor).astype(bf16)
        middle = x + dot(context, w_ref[...])
        middle_ref[0] = middle
        factor = lax.rsqrt(jnp.mean(middle * middle, axis=-1, keepdims=True) + norm_eps)
        normed_ref[0] = (middle * factor * gain_ref[1:2, :]).astype(bf16)

    return run_kernel(
        kernel,
        (batch,),
        [
            token_block(plan),
            whole((2, width)),
            whole((width, width)),
        ]
        + [joined_block(plan, c, index) for c, (_, index) in enumerate(contexts)],
        [token_block(plan)] * 4,
        [struct((batch, pos, width), kind) for kind in (bf16, f32, bf16, bf16)],
        [],
        6,
        tokens,
        gains,
        weights,
        *[values for values, _ in contexts],
    )


def dispatch(plan, which, rows, slots, place):
    cap, tokens, width, n_exp = plan.cap, plan.tokens, plan.width, plan.n_exp

    def kernel(place_ref, slot_ref, row_ref, *out_refs):
        for k, out_ref in enumerate(out_refs):
            first = which * plan.rows + lax.rem(place_ref[0] + k, n_exp) * cap
            slot = first + lax.broadcasted_iota(jnp.int32, (cap, tokens), 0)
            taken = (slot_ref[0:1, :] == slot) | (slot_ref[1:2, :] == slot)
            choice = jnp.where(taken, 1.0, 0.0).astype(bf16)
            out_ref[...] = dot(choice, row_ref[...]).astype(bf16)

    return run_kernel(
        kernel,
        (1,),
        [scalars, whole((2, tokens)), whole((tokens, width))],
        [whole((cap, width))] * n_exp,
        [struct((cap, width), bf16)] * n_exp,
        [],
        5,
        place,
        slots,
        rows,
    )


def dispatch_grads(plan, rows, slots, gates, place):
    cap, tokens, width, n_exp = plan.cap, plan.tokens, plan.width, plan.n_exp

    def kernel(place_ref, slot_ref, gate_ref, row_ref, *out_refs):
        for index, out_ref in enumerate(out_refs):
            group = lax.rem(place_ref[0] + index % n_exp, n_exp)
            first = (index // n_exp) * plan.rows + group * cap
            slot = first + lax.broadcasted_iota(jnp.int32, (cap, tokens), 0)
            taken = [slot_ref[k : k + 1, :] == slot for k in range(2)]
            gate = jnp.where(
                taken[0], gate_ref[0:1, :], jnp.where(taken[1], gate_ref[1:2, :], 0.0)
            )
            gate = jnp.sum(gate, axis=1, keepdims=True)
            choice = jnp.where(taken[0] | taken[1], 1.0, 0.0).astype(bf16)
            out_ref[...] = (dot(choice, row_ref[...]) * gate).astype(bf16)

    made = run_kernel(
        kernel,
        (1,),
        [scalars, whole((2, tokens)), whole((2, tokens)), whole((tokens, width))],
        [whole((cap, width))] * (2 * n_exp),
        [struct((cap, width), bf16)] * (2 * n_exp),
        [],
        8,
        place,
        slots,
        gates,
        rows,
    )
    return made[:n_exp], made[n_exp:]


def pack_expert(matrix_in, matrix_out):
    rows, width = matrix_in.shape[0], matrix_out.shape[1]
    steps = matrix_in.shape[1] // width

    def kernel(in_ref, out_ref, packed_ref):
        for step in range(steps):
            packed_ref[step] = in_ref[:, step * width : (step + 1) * width].astype(bf16)
            packed_ref[steps + step] = out_ref[step * rows : (step + 1) * rows, :].astype(bf16)

    return run_kernel(
        kernel,
        (1,),
        [whole(matrix_in.shape), whole(matrix_out.shape)],
        whole((2 * steps, rows, width)),
        struct((2 * steps, rows, width), bf16),
        [],
        2,
        matrix_in,
        matrix_out,
    )


class ExpertLayout:
    def __init__(self, plan, blocks):
        self.n_seq, count, self.rows, self.width = blocks.shape
        self.steps = count // 2
        self.share = self.n_seq // self.steps
        self.direct = self.rows % 16 == 0
        if self.direct:
            self.operands = [blocks, blocks]
            self.in_spec = pl.BlockSpec(
                (self.n_seq, 1, self.rows, self.width), lambda f: (0, f, 0, 0)
            )
            self.out_spec = pl.BlockSpec(
                (self.share, self.steps, self.rows, self.width), lambda f: (f, 1, 0, 0)
            )
            self.in_tile = (self.n_seq, 1, self.rows, self.width)
            self.out_tile = (self.share, self.steps, self.rows, self.width)
        else:
            tile = (1, 1, self.width, self.width)
            first = blocks[:, : self.steps].transpose(1, 0, 2, 3)
            second = blocks[:, self.steps :]
            shape = (1, self.steps, self.width, self.width)
            self.operands = [first.reshape(shape), second.reshape(shape)]
            self.in_spec = pl.BlockSpec(tile, lambda f: (0, f, 0, 0))
            self.out_spec = self.in_spec


def run_expert(plan, trainable, rows, grads, layout, after):
    cap, width, steps, groups = plan.cap, plan.width, layout.steps, len(rows)
    count = groups * cap

    def kernel(*refs):
        refs = list(refs)

        def next_refs(number):
            return [refs.pop(0) for _ in range(number)]

        x_refs, g_refs, (in_ref, out_ref) = next_refs(groups), next_refs(groups), next_refs(2)
        copy_refs, result_refs = next_refs(groups), next_refs(groups)
        active, active_grad, copy_sum, result_sum = refs
        step = pl.program_id(0)

        @pl.when(step == 0)
        def _():
            copy_sum[...] = jnp.zeros_like(copy_sum)
            result_sum[...] = jnp.zeros_like(result_sum)

        weight_in = in_ref[...].reshape(width, width)
        weight_out = out_ref[...].reshape(width, width)
        for k in range(groups):
            part = slice(k * cap, (k + 1) * cap)
            hidden = dot(x_refs[k][...], weight_in)
            back = dot_rows(g_refs[k][...], weight_out)
            square = hidden * hidden
            bend = jnp.tanh(gelu_scale * hidden * (1.0 + gelu_cubic * square))
            half = 0.5 * (1.0 + bend)
            slope = half + 0.5 * hidden * (1.0 - bend * bend) * (
                gelu_scale + 3.0 * gelu_scale * gelu_cubic * square
            )
            active[part] = (hidden * half).astype(bf16)
            active_grad[part] = (back * slope).astype(bf16)
            copy_sum[part] += dot_rows(active_grad[part], weight_in)
            result_sum[part] += dot(active[part], weight_out)

        @pl.when(step == steps - 1)
        def _():
            for k in range(groups):
                part = slice(k * cap, (k + 1) * cap)
                copy_refs[k][...] = copy_sum[part].astype(bf16)
                result_refs[k][...] = result_sum[part].astype(bf16)

    row_blocks = [whole((cap, width))] * groups
    row_structs = [struct((cap, width), bf16)] * groups
    sums = [pltpu.VMEM((count, width), f32)] * 2
    hidden_specs, hidden_shapes, hidden_scratch = [], [], [pltpu.VMEM((count, width), bf16)] * 2
    if trainable:
        hidden_specs = [pl.BlockSpec((count, width), lambda f: (0, f))] * 2
        hidden_shapes = [struct((count, steps * width), bf16)] * 2
        hidden_scratch = []
    made = run_kernel(
        kernel,
        (steps,),
        row_blocks * 2 + [layout.in_spec, layout.out_spec],
        row_blocks * 2 + hidden_specs,
        row_structs * 2 + hidden_shapes,
        hidden_scratch + sums,
        7 * groups,
        *rows,
        *grads,
        *layout.operands,
        after=after,
    )
    made = list(made)
    return made[:groups], made[groups : 2 * groups], made[2 * groups :]


def expert_weight_grads(plan, rows, grads, hidden, layout, after):
    cap, width, n_exp, count, steps = plan.cap, plan.width, plan.n_exp, plan.rows, layout.steps
    shape = (layout.n_seq, 2 * steps, layout.rows, width)
    parts = len(hidden) // 2

    def kernel(*refs):
        x_refs, g_refs = refs[:n_exp], refs[n_exp : 2 * n_exp]
        hidden_refs, refs = refs[2 * n_exp : 2 * n_exp + 2 * parts], refs[2 * n_exp + 2 * parts :]
        out_ref, rows_t, grads_t = refs
        step = pl.program_id(0)

        @pl.when(step == 0)
        def _():
            for k in range(n_exp):
                rows_t[:, k * cap : (k + 1) * cap] = x_refs[k][...].T
                grads_t[:, k * cap : (k + 1) * cap] = g_refs[k][...].T

        inner, outer, first = 0.0, 0.0, 0
        for part in range(parts):
            active, active_grad = hidden_refs[2 * part : 2 * part + 2]
            span = slice(first, first + active.shape[0])
            inner = inner + dot(rows_t[:, span], active_grad[...])
            outer = outer + dot(grads_t[:, span], active[...])
            first = first + active.shape[0]
        inner, outer = inner.astype(bf16), outer.T.astype(bf16)
        if layout.direct:
            out_ref[:, pl.ds(step, 1)] = inner.reshape(layout.in_tile)
            out_ref[pl.ds(step * layout.share, layout.share), steps:] = outer.reshape(
                layout.out_tile
            )
        else:
            out_ref[0, step] = inner
            out_ref[1, step] = outer

    out_shape = shape if layout.direct else (2, steps, width, width)
    made = run_kernel(
        kernel,
        (steps,),
        [whole((cap, width))] * (2 * n_exp)
        + [pl.BlockSpec((values.shape[0], width), lambda f: (0, f)) for values in hidden],
        whole(out_shape),
        struct(out_shape, bf16),
        [pltpu.VMEM((width, count), bf16)] * 2,
        16,
        *rows,
        *grads,
        *hidden,
        after=after,
    )
    if layout.direct:
        return made
    inner = made[0].reshape(steps, layout.n_seq, layout.rows, width).transpose(1, 0, 2, 3)
    outer = made[1].reshape(layout.n_seq, steps, layout.rows, width)
    return jnp.concatenate([inner, outer], axis=1)


def held_until(values, waited):
    anywhere = pl.BlockSpec(memory_space=pl.ANY)
    held = pl.pallas_call(
        lambda *refs: None,
        in_specs=[anywhere] * (len(values) + len(waited)),
        out_specs=[anywhere] * len(values),
        out_shape=[struct(value.shape, value.dtype) for value in values],
        input_output_aliases={index: index for index in range(len(values))},
        cost_estimate=pl.CostEstimate(flops=0, bytes_accessed=0, transcendentals=0),
    )(*values, *waited)
    return list(held)


def norm_back(values, gain, grad):
    factor = lax.rsqrt(jnp.mean(values * values, axis=-1, keepdims=True) + norm_eps)
    scaled = values * factor
    inner = grad * gain
    slide = jnp.mean(inner * scaled, axis=-1, keepdims=True)
    return (inner - scaled * slide) * factor, jnp.sum(grad * scaled, axis=0, keepdims=True)


def chosen(slot_ref, slots, k):
    index = lax.broadcasted_iota(jnp.int32, (slot_ref.shape[0], slots), 1)
    return slot_ref[:, k : k + 1] == index


def join_rows(refs, joined):
    rows = refs[0].shape[0]
    for index, ref in enumerate(refs):
        joined[index * rows : (index + 1) * rows] = ref[...]


def turn_back(plan, returned, slots, middle, cotangent, context, gains, weights, after):
    batch, pos, width, chunks, cap = plan.batch, plan.pos, plan.width, plan.chunks, plan.cap
    groups = 2 * plan.n_exp

    def kernel(slot_ref, m_ref, y_ref, c_ref, gain_ref, w_ref, *refs):
        back_refs, refs = refs[:groups], refs[groups:]
        grad_ref, output_ref, gain_grad_ref = refs[:3]
        context_grad_refs, (joined, output_sum, gain_sum) = refs[3 : 3 + chunks], refs[3 + chunks :]
        b = pl.program_id(0)

        @pl.when(b == 0)
        def _():
            output_sum[...] = jnp.zeros_like(output_sum)
            gain_sum[...] = jnp.zeros_like(gain_sum)
            join_rows(back_refs, joined)

        choice = chosen(slot_ref, groups * cap, 0) | chosen(slot_ref, groups * cap, 1)
        second_grad = dot(jnp.where(choice, 1.0, 0.0).astype(bf16), joined[...])
        part, gain_grad = norm_back(m_ref[0], gain_ref[1:2, :], second_grad)
        middle_grad = y_ref[0].astype(f32) + part
        grad_ref[0] = middle_grad
        gain_sum[...] += gain_grad
        branch = middle_grad.astype(bf16)
        context_grad = dot_rows(branch, w_ref[...]).astype(bf16)
        for chunk in range(chunks):
            for k, pair in plan.held(chunk):
                if pair < plan.pairs:
                    made = context_grad[:, pair * LANES : (pair + 1) * LANES]
                else:
                    made = jnp.zeros((pos, LANES), bf16)
                context_grad_refs[chunk][k, 0] = made
        output_sum[...] += dot(c_ref[0].T, branch)

        @pl.when(b == batch - 1)
        def _():
            output_ref[:, :width] = output_sum[...].astype(bf16)
            column = jnp.broadcast_to(gain_sum[...], (LANES, width)).T
            output_ref[:, width:] = column.astype(bf16)
            gain_grad_ref[...] = gain_sum[...]

    return run_kernel(
        kernel,
        (batch,),
        [
            pl.BlockSpec((pos, 2), lambda b: (b, 0)),
            token_block(plan),
            token_block(plan),
            token_block(plan),
            whole((2, width)),
            whole((width, width)),
        ]
        + [whole((cap, width))] * groups,
        [token_block(plan), whole((width, width + LANES)), whole((1, width))]
        + [chunk_block(plan, c) for c in range(chunks)],
        [
            struct((batch, pos, width), f32),
            struct((width, width + LANES), bf16),
            struct((1, width), f32),
        ]
        + [struct((plan.per, batch, pos, LANES), bf16)] * chunks,
        [
            pltpu.VMEM((groups * cap, width), bf16),
            pltpu.VMEM((width, width), f32),
            pltpu.VMEM((1, width), f32),
        ],
        12,
        slots,
        middle,
        cotangent,
        context,
        gains,
        weights,
        *returned,
        after=after,
    )


def mix_results(plan, returned, slots, gates, middle, after):
    batch, pos, width, cap = plan.batch, plan.pos, plan.width, plan.cap
    groups = 2 * plan.n_exp

    def kernel(slot_ref, gate_ref, m_ref, *refs):
        back_refs, out_ref, joined = refs[:groups], refs[groups], refs[groups + 1]

        @pl.when(pl.program_id(0) == 0)
        def _():
            join_rows(back_refs, joined)

        total = m_ref[0]
        for k in range(2):
            choice = jnp.where(chosen(slot_ref, groups * cap, k), 1.0, 0.0).astype(bf16)
            total = total + dot(choice, joined[...]) * gate_ref[:, k : k + 1]
        out_ref[0] = total.astype(bf16)

    return run_kernel(
        kernel,
        (batch,),
        [
            pl.BlockSpec((pos, 2), lambda b: (b, 0)),
            pl.BlockSpec((pos, 2), lambda b: (b, 0)),
            token_block(plan),
        ]
        + [whole((cap, width))] * groups,
        token_block(plan),
        struct((batch, pos, width), bf16),
        [pltpu.VMEM((groups * cap, width), bf16)],
        10,
        slots,
        gates,
        middle,
        *returned,
        after=after,
    )


def unit_weight_grads(plan, packed_grads, normed, weights, units, after):
    pos, width, n_seq, chunks = plan.pos, plan.width, plan.n_seq, plan.chunks
    wide = 3 * LANES
    steps = 2
    share = n_seq // steps

    def kernel(unit_ref, *refs):
        g_refs, n_ref, refs = refs[:chunks], refs[chunks], refs[chunks + 1 :]
        w_refs, (out_ref, total, gain_sum) = refs[: 3 * chunks], refs[3 * chunks :]
        step = pl.program_id(1)

        def chunk_step(chunk):
            made = jnp.concatenate(
                [g_refs[chunk][:, part].reshape(share * pos, LANES).T for part in range(3)],
                axis=0,
            )
            made = dot(made, n_ref[:, 0].reshape(share * pos, width))

            @pl.when(step == 0)
            def _():
                total[...] = made

            @pl.when(step == steps - 1)
            def _():
                done = (total[...] + made).T
                out_ref[:, chunk * wide : (chunk + 1) * wide] = done.astype(bf16)
                held = [ref[...].astype(f32) for ref in w_refs[3 * chunk : 3 * chunk + 3]]
                gain = jnp.sum(done * jnp.concatenate(held, axis=1), axis=1, keepdims=True)
                gain = jnp.broadcast_to(gain, (width, LANES))
                if chunk:
                    gain = gain_sum[...] + gain
                gain_sum[...] = gain
                if chunk == chunks - 1:
                    out_ref[:, chunks * wide :] = gain.astype(bf16)

        for chunk in range(chunks):
            pl.when(pl.program_id(0) == chunk)(functools.partial(chunk_step, chunk))

    def grad_block(chunk):
        def place(c, s, unit):
            s = jnp.where(c == chunk, s, jnp.where(c < chunk, 0, steps - 1))
            return (s, 0, 0, 0)

        return pl.BlockSpec((share, 3, pos, LANES), place)

    def weight_block(chunk, part):
        first, used = plan.weight_of(chunk) // LANES, plan.used(chunk)

        def place(c, s, unit):
            return (0, first + part * used + lax.min(unit[chunks], used - 1))

        return pl.BlockSpec((width, LANES), place)

    held = [(chunk, part) for chunk in range(chunks) for part in range(3)]
    out_wide = chunks * wide + LANES
    return run_kernel(
        kernel,
        (chunks, steps),
        [grad_block(chunk) for chunk in range(chunks)]
        + [pl.BlockSpec((share, 1, pos, width), lambda c, s, unit: (s, unit[c], 0, 0))]
        + [weight_block(chunk, part) for chunk, part in held],
        whole((width, out_wide)),
        struct((width, out_wide), bf16),
        [pltpu.VMEM((wide, width), f32), pltpu.VMEM((width, LANES), f32)],
        13,
        *packed_grads,
        normed,
        *[weights] * len(held),
        chosen=[units],
        after=after,
    )


def project_back(plan, packed_grads, tokens, gains, weights, middle_grad):
    batch, pos, width, chunks = plan.batch, plan.pos, plan.width, plan.chunks

    def kernel(x_ref, gain_ref, m_ref, w_ref, *refs):
        g_refs, out_ref = refs[:chunks], refs[chunks]
        first_grad = 0.0
        for chunk in range(chunks):
            used = plan.used(chunk)
            made = jnp.concatenate(
                [g_refs[chunk][k, 0, part] for part in range(3) for k in range(used)], axis=1
            )
            first = plan.weight_of(chunk)
            weight = w_ref[:, first : first + 3 * used * LANES]
            first_grad = first_grad + dot_rows(made, weight)
        piece, _ = norm_back(x_ref[0].astype(f32), gain_ref[0:1, :], first_grad)
        out_ref[0] = m_ref[0] + piece

    def chunk_spec(chunk):
        turn = plan.rolled(chunk)
        return pl.BlockSpec((plan.per, 1, 3, pos, LANES), lambda b: (0, turn(b), 0, 0, 0))

    return run_kernel(
        kernel,
        (batch,),
        [token_block(plan), whole((2, width)), token_block(plan), whole(weights.shape)]
        + [chunk_spec(c) for c in range(chunks)],
        token_block(plan),
        struct((batch, pos, width), f32),
        [],
        10,
        tokens,
        gains,
        middle_grad,
        weights,
        *packed_grads,
    )


def lamb_update(weight, grad, first, second, decay):
    first_new = beta_one * first + (1.0 - beta_one) * grad
    second_new = beta_two * second + (1.0 - beta_two) * grad * grad
    update = (
        first_new
        / (1.0 - beta_one**STEP)
        / (jnp.sqrt(second_new / (1.0 - beta_two**STEP)) + lamb_eps)
        + decay * weight
    )
    return (first_new, second_new, update)


def square_pair(weight, update):
    return jnp.stack([jnp.sum(weight * weight), jnp.sum(update * update)])


def fold_rows(plan, received, output_sums, place, after):
    batch, per, n_exp = plan.batch, plan.per, plan.n_exp
    rows, wide = received.shape[2:]
    other = output_sums.shape[2]

    def kernel(place_ref, r_ref, o_ref, *out_refs):
        for k, out_ref in enumerate(out_refs):
            group = lax.rem(place_ref[0] + k, n_exp)
            for p in range(per):
                total = 0.0
                for b in range(batch):
                    total = total + r_ref[p * batch + b, group].astype(f32)
                out_ref[:, p * wide : (p + 1) * wide] = total.astype(bf16)
            out_ref[:, per * wide :] = o_ref[group]

    return run_kernel(
        kernel,
        (1,),
        [scalars, whole(received.shape), whole(output_sums.shape)],
        [whole((rows, per * wide + other))] * n_exp,
        [struct((rows, per * wide + other), bf16)] * n_exp,
        [],
        3,
        place,
        received,
        output_sums,
        after=after,
    )


def lamb_rows(plan, blocks, weights, known, after):
    n_exp, width, per, chunks = plan.n_exp, plan.width, plan.per, plan.chunks
    rows = blocks[0].shape[0]
    wide = 3 * LANES * chunks + LANES
    devices = plan.n_seq * n_exp
    decays = (decay_rate, decay_rate, 0.0)

    def kernel(*refs):
        block_refs, refs = refs[:n_exp], refs[n_exp:]
        weight_refs, known_ref, refs = refs[:9], refs[9], refs[10:]
        out_refs, sums_ref = refs[:12], refs[12]

        def total(low, high):
            return sum(ref[:, low:high].astype(f32) for ref in block_refs)

        def place_of(part, pair):
            chunk, p = pair // per, pair % per
            return p * wide + (chunk * 3 + part) * LANES

        input_grad = jnp.concatenate(
            [
                total(place_of(part, pair), place_of(part, pair) + LANES)
                for part in range(3)
                for pair in range(plan.pairs)
            ],
            axis=1,
        )
        input_grad = input_grad * weight_refs[6][:, 0:1].astype(bf16).astype(f32)
        first = per * wide
        output_grad = total(first, first + width)
        expert_gain = total(first + width, first + width + LANES)
        attend_gain = sum(total(p * wide + wide - LANES, (p + 1) * wide) for p in range(per))
        gains_grad = jnp.concatenate([attend_gain[:, 0:1], expert_gain[:, 0:1]], axis=1)

        lane = lax.broadcasted_iota(jnp.int32, (1, LANES), 1)
        sums = known_ref[...]
        for index, grad in enumerate((input_grad, output_grad, gains_grad)):
            weight, moment, square = [ref[...] for ref in weight_refs[3 * index : 3 * index + 3]]
            moment, square, update = lamb_update(weight, grad, moment, square, decays[index])
            for ref, value in zip(out_refs[4 * index :], (grad, moment, square, update)):
                ref[...] = value
            for side, value in enumerate((weight, update)):
                parts = [value] if index < 2 else [value[:, 0:1], value[:, 1:2]]
                for part, column in enumerate(parts):
                    found = jnp.sum(column * column, axis=(0, 1), keepdims=True)
                    sums = sums + jnp.where(lane == 2 * (index + part) + side, found, 0.0)
        sums_ref[...] = jnp.broadcast_to(sums[None], sums_ref.shape)

    shapes = [weight.shape for weight in weights]
    outs = [shape for shape in shapes[::3] for _ in range(4)]
    return run_kernel(
        kernel,
        (1,),
        [whole(blocks[0].shape)] * n_exp + [whole(shape) for shape in shapes] + [whole((1, LANES))],
        [whole(shape) for shape in outs] + [whole((devices, 8, LANES))],
        [struct(shape, f32) for shape in outs] + [struct((devices, 8, LANES), f32)],
        [],
        4,
        *blocks,
        *weights,
        known,
        after=after,
    )


def take_step(plan, sums, place, weights, updates):
    n_exp = plan.n_exp
    n_norms = 4 + 2 * n_exp
    count = len(weights)

    def kernel(place_ref, sums_ref, *refs):
        weight_refs, update_refs = refs[:count], refs[count : 2 * count]
        norm_ref, ratio_ref, new_refs = refs[2 * count], refs[2 * count + 1], refs[2 * count + 2 :]
        total = jnp.sum(sums_ref[...], axis=0)
        lane = lax.broadcasted_iota(jnp.int32, total.shape, 1)
        norms = jnp.sqrt(total)
        norm_ref[...] = norms

        def at(values, index):
            return jnp.sum(jnp.where(lane == index, values, 0.0), axis=1, keepdims=True)

        ratios = jnp.where(lane < 2 * n_norms, 0.0, total)
        for index in range(n_norms):
            ratio = at(norms, 2 * index) / at(norms, 2 * index + 1)
            ratios = jnp.where(lane == 2 * index, ratio, ratios)
        ratio_ref[...] = ratios
        own = place_ref[0]
        rates = [at(ratios, 0), at(ratios, 2), None, at(ratios, 8 + 2 * own)]
        rates.append(at(ratios, 8 + 2 * (n_exp + own)))
        for index in range(count):
            update = update_refs[index][...]
            if index == 2:
                first = lax.broadcasted_iota(jnp.int32, update.shape, 1) == 0
                rate = jnp.where(first, at(ratios, 4)[0:1], at(ratios, 6)[0:1])
            else:
                rate = rates[index][0:1]
            new_refs[index][...] = weight_refs[index][...] - learn_rate * rate * update

    row = struct((8, LANES), f32)
    shapes = [weight.shape for weight in weights]
    return run_kernel(
        kernel,
        (1,),
        [scalars, whole(sums.shape)] + [whole(shape) for shape in shapes] * 2,
        [whole(row.shape)] * 2 + [whole(shape) for shape in shapes],
        [row, row] + [struct(shape, f32) for shape in shapes],
        [],
        5,
        place,
        sums,
        *weights,
        *updates,
    )


def body(
    tokens,
    cotangent,
    lengths,
    routes,
    gate_weights,
    norm_gains,
    gains_first,
    gains_second,
    input_weight,
    input_first,
    input_second,
    output_weight,
    output_first,
    output_second,
    frozen_in,
    frozen_out,
    expert_in,
    inner_first,
    inner_second,
    expert_out,
    outer_first,
    outer_second,
):
    plan = Plan(tokens)
    batch, pos, width = plan.batch, plan.pos, plan.width
    seq_place = lax.axis_index("seq")
    exp_place = lax.axis_index("exp")
    seq_lengths = lengths[0]

    input_rows = input_weight.astype(bf16)
    columns = [
        input_rows[:, part * width + pair * LANES : part * width + (pair + 1) * LANES]
        for chunk in range(plan.chunks)
        for part in range(3)
        for _, pair in plan.held(chunk)
        if pair < plan.pairs
    ]
    gain_rows = jnp.pad(norm_gains.astype(bf16), ((0, 0), (0, LANES - 2)))
    row_weights = jnp.concatenate(columns + [gain_rows, output_weight.astype(bf16)], axis=1)
    row_weights = lax.all_gather(row_weights, "exp", axis=0, tiled=True)
    gains_first_column = 3 * width
    split = gains_first_column + LANES
    weights = lax.all_gather(row_weights[:, :split], "seq", axis=0, tiled=True)
    output_low = lax.all_gather(row_weights[:, split:], "seq", axis=0, tiled=True)
    gains = weights[:, gains_first_column : gains_first_column + 2].astype(f32).T

    positions = seq_place * pos + jnp.arange(pos, dtype=jnp.int32)
    live = (positions[None, :] < seq_lengths[:, None]).astype(jnp.int32).reshape(1, plan.tokens)
    slots, counts = routing(plan, routes.reshape(plan.tokens, 2).T, live)
    gate_columns = gate_weights.reshape(plan.tokens, 2)
    place = exp_place.astype(jnp.int32).reshape(1)
    grads_fixed, grads_train = [
        sent(blocks)
        for blocks in dispatch_grads(
            plan, cotangent.reshape(plan.tokens, width), slots, gate_columns.T, place
        )
    ]

    packed = project(plan, tokens, gains, weights, [grads_train[1], grads_train[3]])
    packed = [over_seq(part.reshape(plan.n_seq, 3, pos, LANES)) for part in packed]
    rows = [lax.rem(seq_place + chunk, batch).astype(jnp.int32) for chunk in range(plan.chunks)]
    units = jnp.stack(rows + [(seq_place // batch).astype(jnp.int32)])
    unit_lengths = [lax.dynamic_slice(seq_lengths, (row,), (1,)) for row in rows]
    attended = []
    for c in range(plan.chunks):
        after = [log for _, log in attended[-1:]]
        if c < 2:
            after.append((grads_train, grads_fixed)[c][2])
        attended.append(attend(plan, packed[c], unit_lengths[c], after))

    def joined(parts):
        if not parts:
            return []
        whole_part = over_seq(jnp.stack([p.reshape(plan.n_seq, pos, LANES) for p in parts], axis=1))
        return [(whole_part, index) for index in range(len(parts))]

    def by_pair(part):
        values, index = part
        return values.reshape((plan.per, batch) + values.shape[1:]), index

    contexts = [context for context, _ in attended]
    earlier = joined(contexts[:-1])
    [ending] = held_until(
        contexts[-1:], [values for values, _ in earlier[:1]] + [grads_fixed[1], grads_fixed[3]]
    )
    contexts = [by_pair(part) for part in earlier + joined([ending])]
    context, middle, second_normed, normed = combine_heads(
        plan, tokens, contexts, gains, output_low
    )

    arrived = packed[-1:] + [log for _, log in attended[:-1]]
    train_blocks, fixed_blocks = held_until(
        [pack_expert(expert_in[0], expert_out[0]), pack_expert(frozen_in[0], frozen_out[0])],
        arrived,
    )
    train_layout = ExpertLayout(plan, lax.all_gather(train_blocks, "seq", axis=0))
    fixed_layout = ExpertLayout(plan, lax.all_gather(fixed_blocks, "seq", axis=0))

    normed_rows = second_normed.reshape(plan.tokens, width)
    train_rows = dispatch(plan, 1, normed_rows, slots, place)
    received_train = sent(train_rows)
    fixed_rows = dispatch(plan, 0, normed_rows, slots, place)
    own_copy, own_result, own_hidden = run_expert(
        plan, True, train_rows[:1], grads_train[:1], train_layout, []
    )
    fixed_rows = held_until(fixed_rows, received_train[1:] + own_copy)
    received_fixed = sent(fixed_rows)
    copy_train, result_train, hidden = run_expert(
        plan, True, received_train[1:], grads_train[1:], train_layout, fixed_rows[:1]
    )
    copy_train, result_train = own_copy + copy_train, own_result + result_train
    returned_train = sent_back(copy_train)
    copy_fixed, result_fixed, _ = run_expert(
        plan, False, received_fixed[1:], grads_fixed[1:], fixed_layout, copy_train[1:2]
    )
    own_copy, own_result, _ = run_expert(
        plan, False, received_fixed[:1], grads_fixed[:1], fixed_layout, copy_fixed[:1]
    )
    copy_fixed, result_fixed = own_copy + copy_fixed, own_result + result_fixed
    returned_fixed = sent_back(copy_fixed)
    expert_local = expert_weight_grads(
        plan,
        received_train,
        grads_train,
        own_hidden + hidden,
        train_layout,
        [copy_fixed[0]] + returned_train[1:],
    )
    normed_all = lax.all_gather(normed, "seq", axis=0)

    turned = slots // plan.cap
    turned = jnp.where(
        slots < 0,
        -1,
        (turned // plan.n_exp) * plan.rows
        + ((turned - exp_place) % plan.n_exp) * plan.cap
        + slots % plan.cap,
    ).T
    middle_grad, output_local, gain_expert_grad, *context_grads = turn_back(
        plan,
        returned_fixed + returned_train,
        turned,
        middle,
        cotangent,
        context,
        gains,
        output_low,
        [expert_local, normed_all],
    )
    output_sums = lax.psum_scatter(output_local, "seq", scatter_dimension=0, tiled=True)
    [expert_local] = held_until([expert_local], [normed_all, gain_expert_grad])
    expert_sums = lax.psum_scatter(expert_local, "seq", scatter_dimension=0, tiled=False)
    results = held_until(result_fixed + result_train, [gain_expert_grad])
    results_fixed, results_train = sent_back(results[: plan.n_exp]), sent_back(results[plan.n_exp :])

    context_grads = joined(context_grads[:1]) + joined(context_grads[1:])
    local_grads, packed_grads = [], []
    for c in range(plan.chunks):
        after = local_grads[-1:] if c else [expert_local] + results[:1]
        if c == 1:
            after += results_train[1:2]
        if c == 2:
            after += [packed_grads[0]] + results_train[1:]
        local_grads.append(
            attend_back(
                plan,
                packed[c],
                attended[c][0],
                context_grads[c],
                attended[c][1],
                unit_lengths[c],
                after,
            )
        )
        if c == 0 and plan.chunks > 1:
            local_grads = held_until(local_grads, [context_grads[1][0]])
        if c < plan.chunks - 1:
            packed_grads.append(over_seq(local_grads[c]))

    late = unit_weight_grads(
        plan,
        local_grads,
        normed_all,
        weights,
        units,
        results_fixed[1:] + [output_sums],
    )
    wide = late.shape[1]
    [late] = held_until([late], packed_grads[1:])
    block_output = mix_results(
        plan, results_fixed + results_train, turned, gate_columns, middle, [late]
    )
    late = over_seq(late.reshape(plan.n_seq, -1, wide))
    packed_grads.append(over_seq(held_until(local_grads[-1:], [late])[0]))
    packed_grads = [part.reshape(plan.per, batch, 3, pos, LANES) for part in packed_grads]
    token_grad = project_back(plan, packed_grads, tokens, gains, weights, middle_grad)
    half = expert_sums.shape[0] // 2
    inner_grad = expert_sums[:half].astype(f32).transpose(1, 0, 2).reshape(expert_in.shape)
    outer_grad = expert_sums[half:].astype(f32).reshape(expert_out.shape)
    inner_moment, inner_square, inner_update = lamb_update(
        expert_in, inner_grad, inner_first, inner_second, decay_rate
    )
    outer_moment, outer_square, outer_update = lamb_update(
        expert_out, outer_grad, outer_first, outer_second, decay_rate
    )
    n_norms = 4 + 2 * plan.n_exp
    picker = (jnp.arange(plan.n_exp, dtype=jnp.int32) == exp_place).astype(f32)[:, None]
    known = jnp.concatenate(
        [
            jnp.zeros((8,), f32),
            (picker * square_pair(expert_in, inner_update)[None]).reshape(-1),
            (picker * square_pair(expert_out, outer_update)[None]).reshape(-1),
            counts[:, 0],
            jnp.zeros((LANES - 2 * n_norms - plan.experts,), f32),
        ]
    )[None]
    own_rows = output_weight.shape[0]
    blocks = fold_rows(
        plan,
        late.reshape(plan.n_seq, plan.n_exp, own_rows, wide),
        output_sums.reshape(plan.n_exp, own_rows, -1),
        place,
        [block_output],
    )
    made = lamb_rows(
        plan,
        sent(blocks),
        [
            input_weight,
            input_first,
            input_second,
            output_weight,
            output_first,
            output_second,
            norm_gains,
            gains_first,
            gains_second,
        ],
        known,
        packed_grads[-1:],
    )
    input_grad, input_moment, input_square, input_update = made[:4]
    output_grad, output_moment, output_square, output_update = made[4:8]
    gains_grad, gains_moment, gains_square, gains_update = made[8:12]
    sums = lax.all_to_all(made[12], ("seq", "exp"), split_axis=0, concat_axis=0, tiled=True)
    norms, ratios, input_new, output_new, gains_new, inner_new, outer_new = take_step(
        plan,
        sums,
        place,
        [input_weight, output_weight, norm_gains, expert_in[0], expert_out[0]],
        [input_update, output_update, gains_update, inner_update[0], outer_update[0]],
    )
    inner_new, outer_new = inner_new[None], outer_new[None]
    matrix_norms = norms[0, : 2 * n_norms].reshape(n_norms, 2)
    trust_ratios = ratios[0, : 2 * n_norms].reshape(n_norms, 2)[:, 0]
    routed_counts = ratios[0, 2 * n_norms : 2 * n_norms + plan.experts].astype(jnp.int32)
    return (
        block_output,
        token_grad,
        gains_grad,
        gains_moment,
        gains_square,
        gains_new,
        input_grad,
        input_moment,
        input_square,
        input_new,
        output_grad,
        output_moment,
        output_square,
        output_new,
        inner_grad,
        inner_moment,
        inner_square,
        inner_new,
        outer_grad,
        outer_moment,
        outer_square,
        outer_new,
        matrix_norms,
        trust_ratios,
        routed_counts,
    )


def solution(mesh):
    tokens_spec, rows_spec = P("exp", "seq", None), P(("seq", "exp"), None)
    return jax.shard_map(
        body,
        mesh=mesh,
        in_specs=(
            (tokens_spec,) * 2
            + (P("exp", None),)
            + (tokens_spec,) * 2
            + (rows_spec,) * 9
            + (tokens_spec,) * 8
        ),
        out_specs=(tokens_spec,) * 2 + (rows_spec,) * 12 + (tokens_spec,) * 8 + (P(),) * 3,
        check_vma=False,
    )
```
